768 devices in a mesh: blk: 96 (over x, z_lo, y), grp: 8 (over z_hi, core).
Axes of the slice: x: 4, y: 8, z: 12 (z_hi: 4, z_lo: 3; z = z_hi * 3 + z_lo), core: 2. Of those that a mesh axis runs over, the one named last changes fastest.
Arguments:
- image: bfloat16 [196608, 1152], P(('blk', 'grp')), may hold values from -0.35355339 to 0.35355339
- text: bfloat16 [196608, 1152], P(('blk', 'grp')), may hold values from -0.35355339 to 0.35355339
- exponent_of_multiplier: float32 [1], replicated, may hold values from 4.4 to 4.7
- bias: float32 [1], replicated, may hold values from -13 to -11
Outputs:
- grad_image: float32 [196608, 1152], P(('blk', 'grp'))
- grad_text: float32 [196608, 1152], P(('blk', 'grp'))
- totals: float32 [3], replicated
The draws below stay inside these ranges and needn't reach their ends.
All inputs are finite; a program needn't handle non-finite values.
Results may differ from the reference program's by a relative error of at most 0.0039.
The reference program's roundings to bfloat16 on the way count: a program that leaves them out, or rounds other values in their place, can miss the bound.
Values may be sent and summed in bfloat16 or wider, within the bound.
No kernel may reach another device: no remote copies, remote signals or barrier semaphores. Data moves between devices by JAX's collectives and lax.ppermute only.
A program may use at most 32 MiB of HBM per device.

```python
import math
import jax
import jax.numpy as jnp
from jax import lax

D = 1152
ROWS = 256
STEPS = 4
BATCH = 196608
N_BLK = 96
N_GRP = 8


def noise_rows(key, shape):
    gaussian = jnp.clip(jax.random.normal(jax.random.fold_in(key, 11), shape, jnp.float32), -4.0, 4.0)
    return gaussian * D ** (-0.5)


def shared_rows(key):
    direction = noise_rows(jax.random.fold_in(key, 101), (1, D))
    own_noise = noise_rows(jax.random.fold_in(key, 102), (BATCH, D))
    row_index = jnp.arange(BATCH, dtype=jnp.int32)
    block_count = max(BATCH // ROWS - 1, 1)
    levels = ((row_index // ROWS).astype(jnp.float32) / float(block_count))[:, None]
    common = jnp.sqrt(0.06 * levels) * direction
    return (common, own_noise, levels)


def row_scales(key, lowest, highest):
    return jnp.exp(jax.random.uniform(key, (BATCH, 1), jnp.float32, math.log(lowest), math.log(highest)))


def draw_image(key, part):
    lowest, highest = (0.5, 2.0)
    common, own_noise, levels = shared_rows(key)
    key = jax.random.fold_in(key, 1)
    return (row_scales(key, lowest, highest) * (common + own_noise)).astype(jnp.bfloat16)


def draw_text(key, part):
    lowest, highest = (0.5, 2.0)
    common, own_noise, levels = shared_rows(key)
    key = jax.random.fold_in(key, 2)
    fresh_noise = noise_rows(jax.random.fold_in(key, 1), (BATCH, D))
    jitter = jax.random.uniform(jax.random.fold_in(key, 2), (BATCH, 1), jnp.float32, 0.6, 1.4)
    pairing = (0.22 - 0.14 * levels) * jitter
    scales = row_scales(jax.random.fold_in(key, 3), lowest, highest)
    return (scales * (common + pairing * own_noise + jnp.sqrt(1.0 - pairing * pairing) * fresh_noise)).astype(jnp.bfloat16)


def setup_inputs(seed: int = 0) -> dict:
    arg_keys = jax.random.split(jax.random.key(seed), 5)
    return {
        "image": draw_image(jax.random.fold_in(arg_keys[4], 71), 0),
        "text": draw_text(jax.random.fold_in(arg_keys[4], 71), 0),
        "exponent_of_multiplier": jnp.clip(jax.random.uniform(arg_keys[2], (1,), jnp.float32, 4.4, 4.7), 4.4, 4.7),
        "bias": jnp.clip(jax.random.uniform(arg_keys[3], (1,), jnp.float32, -13.0, -11.0), -13.0, -11.0),
    }


epsilon = 1e-06

def to_unit(values):
    valuef = values.astype(jnp.float32)
    inverse = lax.rsqrt(lax.optimization_barrier(jnp.sum(valuef * valuef, axis=-1, keepdims=True)) + epsilon)
    return (valuef * inverse, inverse)

def reference(image, text, exponent_of_multiplier, bias):
    img_unit, img_inverse = to_unit(image)
    txt_unit, txt_inverse = to_unit(text)
    shape_four = (N_BLK, N_GRP, ROWS, D)
    photo_portion = img_unit.astype(jnp.bfloat16).reshape(shape_four).astype(jnp.float32)
    txt_half = txt_unit.astype(jnp.bfloat16).reshape(shape_four)
    sharpness_factor = jnp.exp(exponent_of_multiplier[0])
    offset_amount = bias[0]
    diagonal_mask = jnp.eye(ROWS, dtype=jnp.float32)
    photo_derivative = jnp.zeros(shape_four, jnp.float32)
    grad_txt = jnp.zeros(shape_four, jnp.float32)
    loss_sum = jnp.float32(0.0)
    multiplier_accumulated = jnp.float32(0.0)
    bias_sum = jnp.float32(0.0)
    for cycle_step in range(STEPS):
        kept_caption = jnp.roll(txt_half, cycle_step, axis=0).astype(jnp.float32)
        cosine_grid = jnp.einsum('bgid,bgjd->bgij', photo_portion, kept_caption)
        pair_score_grid = sharpness_factor * cosine_grid + offset_amount
        if cycle_step == 0:
            desired_polarity = 2.0 * diagonal_mask - 1.0
        else:
            desired_polarity = -jnp.ones((ROWS, ROWS), jnp.float32)
        loss_sum = loss_sum + jnp.sum(jax.nn.softplus(-desired_polarity * pair_score_grid))
        logistic_derivatives = -desired_polarity * jax.nn.sigmoid(-desired_polarity * pair_score_grid)
        multiplier_accumulated = multiplier_accumulated + sharpness_factor * jnp.sum(logistic_derivatives * cosine_grid)
        bias_sum = bias_sum + jnp.sum(logistic_derivatives)
        midpoint_steepness = lax.optimization_barrier(logistic_derivatives.astype(jnp.bfloat16)).astype(jnp.float32)
        photo_derivative = photo_derivative + sharpness_factor * jnp.einsum('jnzi,jnio->jnzo', midpoint_steepness, kept_caption)
        segment_share = sharpness_factor * jnp.einsum('kglo,kgld->kgod', midpoint_steepness, photo_portion)
        grad_txt = grad_txt + jnp.roll(segment_share, -cycle_step, axis=0)
    photo_derivative = photo_derivative.reshape(BATCH, D)
    grad_txt = grad_txt.reshape(BATCH, D)
    grad_image = img_inverse * (photo_derivative - img_unit * lax.optimization_barrier(jnp.sum(img_unit * photo_derivative, axis=-1, keepdims=True)))
    grad_text = txt_inverse * (grad_txt - txt_unit * lax.optimization_barrier(jnp.sum(txt_unit * grad_txt, axis=-1, keepdims=True)))
    pair_count = jnp.float32(BATCH)
    totals = jnp.stack([loss_sum, multiplier_accumulated, bias_sum]) / pair_count
    return (grad_image, grad_text, totals)
```

```python
import jax
import jax.numpy as jnp
from jax import lax
from jax.sharding import Mesh, PartitionSpec as P

EPSILON = 1e-06
BLK_PARTS = (4, 3, 8)
GRP_PARTS = (4, 2)
AXES = ("x", "l", "y", "h", "c")


def hop(value, steps):
    n_blk, n_grp = 96, 8
    pairs = []
    for b in range(n_blk):
        for g in range(n_grp):
            way = steps if g % 2 == 0 else -steps
            pairs.append((b * n_grp + g, ((b + way) % n_blk) * n_grp + g))
    return lax.ppermute(value, AXES, pairs)


def to_unit(values):
    valuef = values.astype(jnp.float32)
    inverse = lax.rsqrt(jnp.sum(valuef * valuef, axis=-1, keepdims=True) + EPSILON)
    return valuef * inverse, inverse


def grid_of(rows, cols):
    return lax.dot_general(rows, cols, (((1,), (1,)), ((), ())), preferred_element_type=jnp.float32)


def slope_of(cosine, scale, offset, z):
    return -z * jax.nn.sigmoid(-z * (scale * cosine + offset))


def sums_of(cosine, scale, offset, z):
    logit = scale * cosine + offset
    slope = -z * jax.nn.sigmoid(-z * logit)
    return jnp.sum(jax.nn.softplus(-z * logit)), jnp.sum(slope * cosine), jnp.sum(slope)


def add3(a, b):
    return tuple(x + y for x, y in zip(a, b))


def summed(value, axes, count):
    out = jnp.broadcast_to(value.reshape(1, 1, 128), (count, 1, 128))
    return jnp.sum(lax.all_to_all(out, axes, 0, 0, tiled=True), axis=0)


def body(image, text, exponent_of_multiplier, bias):
    bar = lax.optimization_barrier
    scale = jnp.exp(exponent_of_multiplier[0])
    offset = bias[0]
    rows = image.shape[0]
    even = lax.axis_index("c") == 0
    p_raw = jnp.where(even, text, image)
    q_raw = jnp.where(even, image, text)
    p_unit, p_inv = to_unit(p_raw)
    p0 = p_unit.astype(jnp.bfloat16)
    p1 = hop(p0, 1)
    q_unit, q_inv = to_unit(q_raw)
    q0 = q_unit.astype(jnp.bfloat16)
    q1 = hop(q0, -1)
    z0 = 2.0 * jnp.eye(rows, dtype=jnp.float32) - 1.0
    z = jnp.float32(-1.0)

    s00 = grid_of(q0, p0)
    sums = sums_of(s00, scale, offset, z0)
    d00 = slope_of(s00, scale, offset, z0).astype(jnp.bfloat16)
    g_q = jnp.dot(d00, p0, preferred_element_type=jnp.float32)
    g_p = lax.dot_general(d00, q0, (((0,), (0,)), ((), ())), preferred_element_type=jnp.float32)
    sums, g_q, g_p, p1, q1 = bar((sums, g_q, g_p, p1, q1))

    p2 = hop(p1, 1)
    s01 = grid_of(q0, p1)
    sums = add3(sums, sums_of(s01, scale, offset, z))
    d01 = slope_of(s01, scale, offset, z).astype(jnp.bfloat16)
    sums = add3(sums, sums_of(grid_of(q1, p1), scale, offset, z))
    d10 = slope_of(grid_of(p0, q1), scale, offset, z).astype(jnp.bfloat16)
    g_q = g_q + jnp.dot(d01, p1, preferred_element_type=jnp.float32)
    g_p = g_p + jnp.dot(d10, q1, preferred_element_type=jnp.float32)
    sums, g_q, g_p, q1s = bar((sums, g_q, g_p, q1))
    q2 = hop(q1s, -1)

    sums = add3(sums, sums_of(grid_of(q1, p2), scale, offset, z))
    sums, p2s = bar((sums, p2))
    p3 = hop(p2s, 1)
    loss, by_scale, by_bias = sums
    row = jnp.concatenate([jnp.stack([loss, scale * by_scale, by_bias]), jnp.zeros((125,), jnp.float32)])
    row = summed(row, ("x", "y", "c"), 64)
    row, q2 = bar((row, q2))
    q3 = hop(q2, -1)
    row, q3, p3 = bar((summed(row, ("l", "h"), 12), q3, p3))
    pair_count = jnp.float32(rows * 768)
    totals = row.reshape(128)[:3] / pair_count

    d02 = slope_of(grid_of(q0, p2), scale, offset, z).astype(jnp.bfloat16)
    d20 = slope_of(grid_of(p0, q2), scale, offset, z).astype(jnp.bfloat16)
    d03 = slope_of(grid_of(q0, p3), scale, offset, z).astype(jnp.bfloat16)
    d30 = slope_of(grid_of(p0, q3), scale, offset, z).astype(jnp.bfloat16)
    g_q = g_q + jnp.dot(d02, p2, preferred_element_type=jnp.float32)
    g_p = g_p + jnp.dot(d20, q2, preferred_element_type=jnp.float32)
    g_q = g_q + jnp.dot(d03, p3, preferred_element_type=jnp.float32)
    g_p = g_p + jnp.dot(d30, q3, preferred_element_type=jnp.float32)
    g_q = scale * g_q
    g_p = scale * g_p
    grad_q = q_inv * (g_q - q_unit * jnp.sum(q_unit * g_q, axis=-1, keepdims=True))
    grad_p = p_inv * (g_p - p_unit * jnp.sum(p_unit * g_p, axis=-1, keepdims=True))
    return jnp.where(even, grad_q, grad_p), jnp.where(even, grad_p, grad_q), totals


def solution(mesh):
    fine = Mesh(mesh.devices.reshape(BLK_PARTS + GRP_PARTS), AXES)
    split = P(AXES, None)
    return jax.shard_map(
        body,
        mesh=fine,
        in_specs=(split, split, P(), P()),
        out_specs=(split, split, P()),
        check_vma=False,
    )
```

```python
import functools

import jax
import jax.numpy as jnp
from jax import lax
from jax.experimental import pallas as pl
from jax.experimental.pallas import tpu as pltpu
from jax.sharding import Mesh, PartitionSpec as P

EPSILON = 1e-06
ROWS, D = 256, 1152
BLK_PARTS = (4, 3, 8)
GRP_PARTS = (4, 2)
N_BLK, N_GRP = 96, 8
AXES = ("x", "l", "y", "h", "c")
BF16, F32 = jnp.bfloat16, jnp.float32
PARAMS = pltpu.CompilerParams(vmem_limit_bytes=40 * 1024 * 1024)
CHUNK = 32

SMEM = pl.BlockSpec(memory_space=pltpu.SMEM)
VMEM = pl.BlockSpec(memory_space=pltpu.VMEM)
ANY = pl.BlockSpec(memory_space=pl.ANY)


def hop(value, steps):
    pairs = []
    for b in range(N_BLK):
        for g in range(N_GRP):
            way = steps if g % 2 == 0 else -steps
            pairs.append((b * N_GRP + g, ((b + way) % N_BLK) * N_GRP + g))
    return lax.ppermute(value, AXES, pairs)


def cosines(rows, cols):
    return lax.dot_general(rows, cols, (((1,), (1,)), ((), ())), preferred_element_type=F32)


def sigmoid_parts(x):
    small = jnp.exp(-jnp.abs(x))
    return small, jnp.where(x >= 0, 1.0, small) / (1.0 + small)


def folded(values):
    part = values[0:8]
    for r in range(8, ROWS, 8):
        part = part + values[r : r + 8]
    return part[:, 0:128] + part[:, 128:256]


def add_sums(sums_ref, cosine, logit, x, slope, small):
    softplus = jnp.maximum(x, 0.0) + jnp.log1p(small)
    sums_ref[0:8, :] += folded(softplus)
    sums_ref[8:16, :] += folded(slope * cosine)
    sums_ref[16:24, :] += folded(slope)


def logits(cosine, e_ref, b_ref):
    scale = jnp.exp(jnp.full((1, ROWS), e_ref[0], F32))
    return scale * cosine + b_ref[0]


def to_unit(source, out):
    for r in range(0, ROWS, CHUNK):
        v = source[r : r + CHUNK, :].astype(F32)
        inverse = lax.rsqrt(jnp.sum(v * v, axis=-1, keepdims=True) + EPSILON)
        out[r : r + CHUNK, :] = (v * inverse).astype(BF16)


def unit_kernel(image, text, p0, q0):
    even = lax.axis_index("c") == 0

    @pl.when(even)
    def _():
        to_unit(text, p0)
        to_unit(image, q0)

    @pl.when(jnp.logical_not(even))
    def _():
        to_unit(image, p0)
        to_unit(text, q0)


def units(image, text):
    rows = jax.ShapeDtypeStruct((ROWS, D), BF16)
    return pl.pallas_call(
        unit_kernel,
        out_shape=(rows, rows),
        in_specs=[VMEM, VMEM],
        out_specs=(VMEM, VMEM),
        compiler_params=PARAMS,
        cost_estimate=pl.CostEstimate(flops=2 * 10**6, bytes_accessed=2400000, transcendentals=512),
    )(image, text)


def own_kernel(e_ref, b_ref, p0, q0, d00, d00t, sums):
    i = lax.broadcasted_iota(jnp.int32, (ROWS, ROWS), 0)
    j = lax.broadcasted_iota(jnp.int32, (ROWS, ROWS), 1)
    pair = i == j
    sums[...] = jnp.zeros_like(sums)
    cosine = cosines(q0[...], p0[...])
    logit = logits(cosine, e_ref, b_ref)
    x = jnp.where(pair, -logit, logit)
    small, sig = sigmoid_parts(x)
    slope = jnp.where(pair, -sig, sig)
    add_sums(sums, cosine, logit, x, slope, small)
    d00[...] = slope.astype(BF16)
    logit = logits(cosines(p0[...], q0[...]), e_ref, b_ref)
    _, sig = sigmoid_parts(jnp.where(pair, -logit, logit))
    d00t[...] = jnp.where(pair, -sig, sig).astype(BF16)


def own(e, b, p0, q0):
    return pl.pallas_call(
        own_kernel,
        out_shape=(
            jax.ShapeDtypeStruct((ROWS, ROWS), BF16),
            jax.ShapeDtypeStruct((ROWS, ROWS), BF16),
            jax.ShapeDtypeStruct((24, 128), F32),
        ),
        in_specs=[SMEM, SMEM, VMEM, VMEM],
        out_specs=(VMEM, VMEM, VMEM),
        compiler_params=PARAMS,
        cost_estimate=pl.CostEstimate(flops=3 * 10**8, bytes_accessed=1500000, transcendentals=200000),
    )(e, b, p0, q0)


def middle_kernel(e_ref, b_ref, sums_in, p0, q0, p1, q1, d01, d10, sums):
    sums[...] = sums_in[...]
    cosine = cosines(q0[...], p1[...])
    logit = logits(cosine, e_ref, b_ref)
    small, slope = sigmoid_parts(logit)
    add_sums(sums, cosine, logit, logit, slope, small)
    d01[...] = slope.astype(BF16)
    cosine = cosines(q1[...], p1[...])
    logit = logits(cosine, e_ref, b_ref)
    small, slope = sigmoid_parts(logit)
    add_sums(sums, cosine, logit, logit, slope, small)
    _, slope = sigmoid_parts(logits(cosines(p0[...], q1[...]), e_ref, b_ref))
    d10[...] = slope.astype(BF16)


def middle(e, b, sums, p0, q0, p1, q1):
    return pl.pallas_call(
        middle_kernel,
        out_shape=(
            jax.ShapeDtypeStruct((ROWS, ROWS), BF16),
            jax.ShapeDtypeStruct((ROWS, ROWS), BF16),
            jax.ShapeDtypeStruct((24, 128), F32),
        ),
        in_specs=[SMEM, SMEM] + [VMEM] * 5,
        out_specs=(VMEM, VMEM, VMEM),
        compiler_params=PARAMS,
        cost_estimate=pl.CostEstimate(flops=5 * 10**8, bytes_accessed=2700000, transcendentals=300000),
    )(e, b, sums, p0, q0, p1, q1)


def last_kernel(e_ref, b_ref, sums_in, q1, p2, out, sums):
    sums[...] = sums_in[...]
    cosine = cosines(q1[...], p2[...])
    logit = logits(cosine, e_ref, b_ref)
    small, slope = sigmoid_parts(logit)
    add_sums(sums, cosine, logit, logit, slope, small)
    scale = jnp.exp(jnp.full((1, 1), e_ref[0], F32))
    loss = jnp.sum(sums[0:8, :], keepdims=True)
    by_scale = scale * jnp.sum(sums[8:16, :], keepdims=True)
    by_bias = jnp.sum(sums[16:24, :], keepdims=True)
    lane = lax.broadcasted_iota(jnp.int32, out.shape, 1)
    row = jnp.where(lane == 0, loss, jnp.where(lane == 1, by_scale, jnp.where(lane == 2, by_bias, 0.0)))
    out[...] = row


def last(e, b, sums, q1, p2, count):
    return pl.pallas_call(
        last_kernel,
        out_shape=jax.ShapeDtypeStruct((count, 128), F32),
        in_specs=[SMEM, SMEM] + [VMEM] * 3,
        out_specs=VMEM,
        scratch_shapes=[pltpu.VMEM((24, 128), F32)],
        compiler_params=PARAMS,
        cost_estimate=pl.CostEstimate(flops=2 * 10**8, bytes_accessed=1200000, transcendentals=100000),
    )(e, b, sums, q1, p2)


def block(k):
    return pl.ds(k * ROWS, ROWS)


def started(pairs, sems):
    copies = [pltpu.make_async_copy(src, dst, sems.at[n]) for n, (src, dst) in enumerate(pairs)]
    for copy in copies:
        copy.start()
    return copies


def either(chosen, first, second):
    @pl.when(chosen)
    def _():
        first.start()

    @pl.when(jnp.logical_not(chosen))
    def _():
        second.start()


def finish(e_ref, slopes, others, raw, out):
    scale = jnp.exp(jnp.full((1, 1), e_ref[0], F32))
    out[...] = jnp.dot(slopes[...], others[...], preferred_element_type=F32)
    for r in range(0, ROWS, CHUNK):
        rows = slice(r, r + CHUNK)
        v = raw[rows, :].astype(F32)
        inverse = lax.rsqrt(jnp.sum(v * v, axis=-1, keepdims=True) + EPSILON)
        u = v * inverse
        g = scale * out[rows, :]
        out[rows, :] = inverse * (g - u * jnp.sum(u * g, axis=-1, keepdims=True))


def slope_block(e_ref, b_ref, rows, cols):
    return sigmoid_parts(logits(cosines(rows, cols), e_ref, b_ref))[1].astype(BF16)


def q_kernel(early_call, e_ref, b_ref, image, text, p0, p1, p2, p3, q0, q2, d00, d01, *refs):
    out_image, out_text, d20, y, own, other, d, cross, raw, out, sems, out_sems = refs if early_call else refs[3:]
    early = jnp.logical_and(lax.axis_index("h") == 0, lax.axis_index("l") < 2)
    is_text = lax.axis_index("c") == 1
    mine = early if early_call else jnp.logical_not(early)

    @pl.when(mine)
    def _():
        copies = started(
            [
                (q0, own),
                (p2, y.at[block(2), :]),
                (p3, y.at[block(3), :]),
                (p0, y.at[block(0), :]),
                (q2, other),
                (p1, y.at[block(1), :]),
                (d00, d.at[:, block(0)]),
                (d01, d.at[:, block(1)]),
            ],
            sems,
        )
        from_text = pltpu.make_async_copy(text, raw, sems.at[8])
        from_image = pltpu.make_async_copy(image, raw, sems.at[8])
        either(is_text, from_text, from_image)
        copies[0].wait()
        for k in (2, 3):
            copies[k - 1].wait()
            d[:, block(k)] = slope_block(e_ref, b_ref, own[...], y[block(k), :])
        copies[3].wait()
        copies[4].wait()
        cross[...] = slope_block(e_ref, b_ref, y[block(0), :], other[...])
        cross_copy = pltpu.make_async_copy(cross, d20, out_sems.at[0])
        cross_copy.start()
        for copy in copies[5:]:
            copy.wait()
        from_text.wait()
        finish(e_ref, d, y, raw, out)
        to_text = pltpu.make_async_copy(out, out_text, out_sems.at[1])
        either(is_text, to_text, pltpu.make_async_copy(out, out_image, out_sems.at[1]))
        cross_copy.wait()
        to_text.wait()


def p_kernel(e_ref, b_ref, image, text, q0, q1, q2, q3, p0, d00t, d10, d20, *refs):
    _, _, out_image, out_text, y, own, d, raw, out, sems, out_sem = refs
    is_text = lax.axis_index("c") == 0
    copies = started(
        [
            (p0, own),
            (q3, y.at[block(3), :]),
            (q0, y.at[block(0), :]),
            (q1, y.at[block(1), :]),
            (q2, y.at[block(2), :]),
            (d00t, d.at[:, block(0)]),
            (d10, d.at[:, block(1)]),
            (d20, d.at[:, block(2)]),
        ],
        sems,
    )
    from_text = pltpu.make_async_copy(text, raw, sems.at[8])
    from_image = pltpu.make_async_copy(image, raw, sems.at[8])
    either(is_text, from_text, from_image)
    copies[0].wait()
    copies[1].wait()
    d[:, block(3)] = slope_block(e_ref, b_ref, own[...], y[block(3), :])
    for copy in copies[2:]:
        copy.wait()
    from_text.wait()
    finish(e_ref, d, y, raw, out)
    to_text = pltpu.make_async_copy(out, out_text, out_sem)
    either(is_text, to_text, pltpu.make_async_copy(out, out_image, out_sem))
    to_text.wait()


GRAD = jax.ShapeDtypeStruct((ROWS, D), F32)
SLOPES = jax.ShapeDtypeStruct((ROWS, ROWS), BF16)


def q_side(args, previous):
    early_call = previous is None
    n = len(args)
    return pl.pallas_call(
        functools.partial(q_kernel, early_call),
        out_shape=(GRAD, GRAD, SLOPES),
        in_specs=[SMEM, SMEM] + [ANY] * (n - 2 + (0 if early_call else 3)),
        out_specs=(ANY, ANY, ANY),
        input_output_aliases={} if early_call else {n: 0, n + 1: 1, n + 2: 2},
        scratch_shapes=[
            pltpu.VMEM((4 * ROWS, D), BF16),
            pltpu.VMEM((ROWS, D), BF16),
            pltpu.VMEM((ROWS, D), BF16),
            pltpu.VMEM((ROWS, 4 * ROWS), BF16),
            pltpu.VMEM((ROWS, ROWS), BF16),
            pltpu.VMEM((ROWS, D), BF16),
            pltpu.VMEM((ROWS, D), F32),
            pltpu.SemaphoreType.DMA((9,)),
            pltpu.SemaphoreType.DMA((2,)),
        ],
        compiler_params=PARAMS,
        cost_estimate=pl.CostEstimate(flops=10**9, bytes_accessed=5000000, transcendentals=200000),
    )(*args, *([] if early_call else previous))


def p_side(args, previous):
    n = len(args)
    return pl.pallas_call(
        p_kernel,
        out_shape=(GRAD, GRAD),
        in_specs=[SMEM, SMEM] + [ANY] * n,
        out_specs=(ANY, ANY),
        input_output_aliases={n: 0, n + 1: 1},
        scratch_shapes=[
            pltpu.VMEM((4 * ROWS, D), BF16),
            pltpu.VMEM((ROWS, D), BF16),
            pltpu.VMEM((ROWS, 4 * ROWS), BF16),
            pltpu.VMEM((ROWS, D), BF16),
            pltpu.VMEM((ROWS, D), F32),
            pltpu.SemaphoreType.DMA((9,)),
            pltpu.SemaphoreType.DMA,
        ],
        compiler_params=PARAMS,
        cost_estimate=pl.CostEstimate(flops=10**9, bytes_accessed=5000000, transcendentals=200000),
    )(*args, *previous)


def body(image, text, e, b):
    bar = lax.optimization_barrier
    p0, q0 = units(image, text)
    p1 = hop(p0, 1)
    q1 = hop(q0, -1)
    d00, d00t, sums = own(e, b, p0, q0)
    sums, p1, q1 = bar((sums, p1, q1))

    p2 = hop(p1, 1)
    d01, d10, sums = middle(e, b, sums, p0, q0, p1, q1)
    sums, q1s = bar((sums, q1))
    q2 = hop(q1s, -1)
    row = last(e, b, sums, q1, p2, 64)
    row, p2s = bar((row, p2))
    p3 = hop(p2s, 1)
    row = lax.all_to_all(row, ("x", "y", "c"), 0, 0, tiled=True)
    row, q2s = bar((row, q2))
    q3 = hop(q2s, -1)
    row = jnp.sum(row, axis=0, keepdims=True)
    q_args = (e, b, image, text, p0, p1, p2, p3, q0, q2s, d00, d01)
    row, done = bar((row, q_side(q_args, None)))
    row = lax.all_to_all(jnp.broadcast_to(row, (12, 128)), ("l", "h"), 0, 0, tiled=True)
    row, done = bar((row, done))
    totals = jnp.sum(row, axis=0)[:3] / jnp.float32(ROWS * N_BLK * N_GRP)
    grad_image, grad_text, d20 = q_side(q_args, done)
    p_args = (e, b, image, text, q0, q1, q2s, q3, p0, d00t, d10, d20)
    grad_image, grad_text = p_side(p_args, (grad_image, grad_text))
    return grad_image, grad_text, totals


def solution(mesh):
    fine = Mesh(mesh.devices.reshape(BLK_PARTS + GRP_PARTS), AXES)
    split = P(AXES, None)
    return jax.shard_map(
        body,
        mesh=fine,
        in_specs=(split, split, P(), P()),
        out_specs=(split, split, P()),
        check_vma=False,
    )
```

```python
import functools

import jax
import jax.numpy as jnp
from jax import lax
from jax.experimental import pallas as pl
from jax.experimental.pallas import tpu as pltpu
from jax.sharding import Mesh, PartitionSpec as P

EPSILON = 1e-06
ROWS, D = 256, 1152
BLK_PARTS = (4, 3, 8)
GRP_PARTS = (4, 2)
N_BLK, N_GRP = 96, 8
AXES = ("x", "l", "y", "h", "c")
BF16, F32 = jnp.bfloat16, jnp.float32
PARAMS = pltpu.CompilerParams(vmem_limit_bytes=16 * 1024 * 1024)
WHOLE = pltpu.CompilerParams(vmem_limit_bytes=60 * 1024 * 1024)
CHUNK = 32
EARLY_PLANES = 5

SMEM = pl.BlockSpec(memory_space=pltpu.SMEM)
VMEM = pl.BlockSpec(memory_space=pltpu.VMEM)
HBM = pl.BlockSpec(memory_space=pltpu.HBM)


def hop(value, steps):
    pairs = []
    for b in range(N_BLK):
        for g in range(N_GRP):
            way = steps if g % 2 == 0 else -steps
            pairs.append((b * N_GRP + g, ((b + way) % N_BLK) * N_GRP + g))
    return lax.ppermute(value, AXES, pairs)


def cosines(rows, cols):
    return lax.dot_general(rows, cols, (((1,), (1,)), ((), ())), preferred_element_type=F32)


def sigmoid_parts(x):
    small = jnp.exp(-jnp.abs(x))
    return small, jnp.where(x >= 0, 1.0, small) / (1.0 + small)


def folded(values):
    part = values[0:8]
    for r in range(8, ROWS, 8):
        part = part + values[r : r + 8]
    return part[:, 0:128] + part[:, 128:256]


def add_sums(sums_ref, cosine, logit, x, slope, small):
    softplus = jnp.maximum(x, 0.0) + jnp.log1p(small)
    sums_ref[0:8, :] += folded(softplus)
    sums_ref[8:16, :] += folded(slope * cosine)
    sums_ref[16:24, :] += folded(slope)


def logits(cosine, e_ref, b_ref):
    scale = jnp.exp(jnp.full((1, ROWS), e_ref[0], F32))
    return scale * cosine + b_ref[0]


PART = 64


def unit_kernel(image, text, p0, q0, raw, sems):
    even = lax.axis_index("c") == 0
    loads = {}
    for name, source in (("image", image), ("text", text)):
        for side in range(2):
            for n in range(ROWS // PART):
                rows = pl.ds(n * PART, PART)
                loads[name, side, n] = pltpu.make_async_copy(
                    source.at[rows, :], raw.at[side, rows, :], sems.at[side, n]
                )

    @pl.when(even)
    def _():
        for n in range(ROWS // PART):
            loads["text", 0, n].start()
        for n in range(ROWS // PART):
            loads["image", 1, n].start()

    @pl.when(jnp.logical_not(even))
    def _():
        for n in range(ROWS // PART):
            loads["image", 0, n].start()
        for n in range(ROWS // PART):
            loads["text", 1, n].start()

    for side, out in enumerate((p0, q0)):
        for n in range(ROWS // PART):
            loads["image", side, n].wait()
            for r in range(n * PART, (n + 1) * PART, CHUNK):
                v = raw[side, r : r + CHUNK, :].astype(F32)
                inverse = lax.rsqrt(jnp.sum(v * v, axis=-1, keepdims=True) + EPSILON)
                out[r : r + CHUNK, :] = (v * inverse).astype(BF16)


def units(image, text):
    rows = jax.ShapeDtypeStruct((ROWS, D), BF16)
    return pl.pallas_call(
        unit_kernel,
        out_shape=(rows, rows),
        in_specs=[HBM, HBM],
        out_specs=(VMEM, VMEM),
        scratch_shapes=[pltpu.VMEM((2, ROWS, D), BF16), pltpu.SemaphoreType.DMA((2, ROWS // PART))],
        compiler_params=WHOLE,
        cost_estimate=pl.CostEstimate(flops=2 * 10**6, bytes_accessed=2400000, transcendentals=512),
    )(image, text)


def own_kernel(e_ref, b_ref, p0, q0, d00, d00t, sums):
    i = lax.broadcasted_iota(jnp.int32, (ROWS, ROWS), 0)
    j = lax.broadcasted_iota(jnp.int32, (ROWS, ROWS), 1)
    pair = i == j
    sums[...] = jnp.zeros_like(sums)
    cosine = cosines(q0[...], p0[...])
    logit = logits(cosine, e_ref, b_ref)
    x = jnp.where(pair, -logit, logit)
    small, sig = sigmoid_parts(x)
    slope = jnp.where(pair, -sig, sig)
    add_sums(sums, cosine, logit, x, slope, small)
    d00[...] = slope.astype(BF16)
    logit = logits(cosines(p0[...], q0[...]), e_ref, b_ref)
    _, sig = sigmoid_parts(jnp.where(pair, -logit, logit))
    d00t[...] = jnp.where(pair, -sig, sig).astype(BF16)


def own(e, b, p0, q0):
    return pl.pallas_call(
        own_kernel,
        out_shape=(
            jax.ShapeDtypeStruct((ROWS, ROWS), BF16),
            jax.ShapeDtypeStruct((ROWS, ROWS), BF16),
            jax.ShapeDtypeStruct((24, 128), F32),
        ),
        in_specs=[SMEM, SMEM, VMEM, VMEM],
        out_specs=(VMEM, VMEM, VMEM),
        compiler_params=PARAMS,
        cost_estimate=pl.CostEstimate(flops=3 * 10**8, bytes_accessed=1500000, transcendentals=200000),
    )(e, b, p0, q0)


def middle_kernel(e_ref, b_ref, sums_in, p0, q0, p1, q1, d01, d10, sums):
    sums[...] = sums_in[...]
    cosine = cosines(q0[...], p1[...])
    logit = logits(cosine, e_ref, b_ref)
    small, slope = sigmoid_parts(logit)
    add_sums(sums, cosine, logit, logit, slope, small)
    d01[...] = slope.astype(BF16)
    cosine = cosines(q1[...], p1[...])
    logit = logits(cosine, e_ref, b_ref)
    small, slope = sigmoid_parts(logit)
    add_sums(sums, cosine, logit, logit, slope, small)
    _, slope = sigmoid_parts(logits(cosines(p0[...], q1[...]), e_ref, b_ref))
    d10[...] = slope.astype(BF16)


def middle(e, b, sums, p0, q0, p1, q1):
    return pl.pallas_call(
        middle_kernel,
        out_shape=(
            jax.ShapeDtypeStruct((ROWS, ROWS), BF16),
            jax.ShapeDtypeStruct((ROWS, ROWS), BF16),
            jax.ShapeDtypeStruct((24, 128), F32),
        ),
        in_specs=[SMEM, SMEM] + [VMEM] * 5,
        out_specs=(VMEM, VMEM, VMEM),
        compiler_params=PARAMS,
        cost_estimate=pl.CostEstimate(flops=5 * 10**8, bytes_accessed=2700000, transcendentals=300000),
    )(e, b, sums, p0, q0, p1, q1)


def last_kernel(e_ref, b_ref, sums_in, q1, p2, out, sums):
    sums[...] = sums_in[...]
    cosine = cosines(q1[...], p2[...])
    logit = logits(cosine, e_ref, b_ref)
    small, slope = sigmoid_parts(logit)
    add_sums(sums, cosine, logit, logit, slope, small)
    scale = jnp.exp(jnp.full((1, 1), e_ref[0], F32))
    loss = jnp.sum(sums[0:8, :], keepdims=True)
    by_scale = scale * jnp.sum(sums[8:16, :], keepdims=True)
    by_bias = jnp.sum(sums[16:24, :], keepdims=True)
    lane = lax.broadcasted_iota(jnp.int32, out.shape, 1)
    row = jnp.where(lane == 0, loss, jnp.where(lane == 1, by_scale, jnp.where(lane == 2, by_bias, 0.0)))
    out[...] = row


def last(e, b, sums, q1, p2, count):
    return pl.pallas_call(
        last_kernel,
        out_shape=jax.ShapeDtypeStruct((count, 128), F32),
        in_specs=[SMEM, SMEM] + [VMEM] * 3,
        out_specs=VMEM,
        scratch_shapes=[pltpu.VMEM((24, 128), F32)],
        compiler_params=PARAMS,
        cost_estimate=pl.CostEstimate(flops=2 * 10**8, bytes_accessed=1200000, transcendentals=100000),
    )(e, b, sums, q1, p2)


def block(k):
    return pl.ds(k * ROWS, ROWS)


def started(pairs, sems):
    copies = [pltpu.make_async_copy(src, dst, sems.at[n]) for n, (src, dst) in enumerate(pairs)]
    for copy in copies:
        copy.start()
    return copies


def either(chosen, first, second):
    @pl.when(chosen)
    def _():
        first.start()

    @pl.when(jnp.logical_not(chosen))
    def _():
        second.start()


def finish(e_ref, slopes, others, raw, out, is_text, out_image, out_text, sem):
    scale = jnp.exp(jnp.full((1, 1), e_ref[0], F32))
    out[...] = jnp.dot(slopes[...], others[...], preferred_element_type=F32)
    for r in range(0, ROWS, CHUNK):
        rows = slice(r, r + CHUNK)
        v = raw[rows, :].astype(F32)
        inverse = lax.rsqrt(jnp.sum(v * v, axis=-1, keepdims=True) + EPSILON)
        u = v * inverse
        g = scale * out[rows, :]
        out[rows, :] = inverse * (g - u * jnp.sum(u * g, axis=-1, keepdims=True))
        if (r + CHUNK) % PART == 0:
            part = pl.ds(r + CHUNK - PART, PART)
            either(
                is_text,
                pltpu.make_async_copy(out.at[part, :], out_text.at[part, :], sem),
                pltpu.make_async_copy(out.at[part, :], out_image.at[part, :], sem),
            )
    pltpu.make_async_copy(out, out_text, sem).wait()


def slope_block(e_ref, b_ref, rows, cols):
    return sigmoid_parts(logits(cosines(rows, cols), e_ref, b_ref))[1].astype(BF16)


def q_kernel(early_call, e_ref, b_ref, image, text, p0, p1, p2, p3, q0, q2, d00, d01, *refs):
    out_image, out_text, d20, y, own, other, d, cross, raw, out, sems, out_sems = refs if early_call else refs[3:]
    early = 3 * lax.axis_index("h") + lax.axis_index("l") < EARLY_PLANES
    is_text = lax.axis_index("c") == 1
    mine = early if early_call else jnp.logical_not(early)

    @pl.when(mine)
    def _():
        copies = started(
            [
                (q0, own),
                (p2, y.at[block(2), :]),
                (p3, y.at[block(3), :]),
                (p0, y.at[block(0), :]),
                (q2, other),
                (p1, y.at[block(1), :]),
                (d00, d.at[:, block(0)]),
                (d01, d.at[:, block(1)]),
            ],
            sems,
        )
        from_text = pltpu.make_async_copy(text, raw, sems.at[8])
        from_image = pltpu.make_async_copy(image, raw, sems.at[8])
        either(is_text, from_text, from_image)
        copies[0].wait()
        for k in (2, 3):
            copies[k - 1].wait()
            d[:, block(k)] = slope_block(e_ref, b_ref, own[...], y[block(k), :])
        copies[3].wait()
        copies[4].wait()
        cross[...] = slope_block(e_ref, b_ref, y[block(0), :], other[...])
        cross_copy = pltpu.make_async_copy(cross, d20, out_sems.at[0])
        cross_copy.start()
        for copy in copies[5:]:
            copy.wait()
        from_text.wait()
        finish(e_ref, d, y, raw, out, is_text, out_image, out_text, out_sems.at[1])
        cross_copy.wait()


def p_kernel(e_ref, b_ref, image, text, q0, q1, q2, q3, p0, d00t, d10, d20, *refs):
    _, _, out_image, out_text, y, own, d, raw, out, sems, out_sem = refs
    is_text = lax.axis_index("c") == 0
    copies = started(
        [
            (p0, own),
            (q3, y.at[block(3), :]),
            (q0, y.at[block(0), :]),
            (q1, y.at[block(1), :]),
            (q2, y.at[block(2), :]),
            (d00t, d.at[:, block(0)]),
            (d10, d.at[:, block(1)]),
            (d20, d.at[:, block(2)]),
        ],
        sems,
    )
    from_text = pltpu.make_async_copy(text, raw, sems.at[8])
    from_image = pltpu.make_async_copy(image, raw, sems.at[8])
    either(is_text, from_text, from_image)
    copies[0].wait()
    copies[1].wait()
    d[:, block(3)] = slope_block(e_ref, b_ref, own[...], y[block(3), :])
    for copy in copies[2:]:
        copy.wait()
    from_text.wait()
    finish(e_ref, d, y, raw, out, is_text, out_image, out_text, out_sem)


GRAD = jax.ShapeDtypeStruct((ROWS, D), F32)
SLOPES = jax.ShapeDtypeStruct((ROWS, ROWS), BF16)


def q_side(args, previous):
    early_call = previous is None
    n = len(args)
    return pl.pallas_call(
        functools.partial(q_kernel, early_call),
        out_shape=(GRAD, GRAD, SLOPES),
        in_specs=[SMEM, SMEM] + [HBM] * (n - 2 + (0 if early_call else 3)),
        out_specs=(HBM, HBM, HBM),
        input_output_aliases={} if early_call else {n: 0, n + 1: 1, n + 2: 2},
        scratch_shapes=[
            pltpu.VMEM((4 * ROWS, D), BF16),
            pltpu.VMEM((ROWS, D), BF16),
            pltpu.VMEM((ROWS, D), BF16),
            pltpu.VMEM((ROWS, 4 * ROWS), BF16),
            pltpu.VMEM((ROWS, ROWS), BF16),
            pltpu.VMEM((ROWS, D), BF16),
            pltpu.VMEM((ROWS, D), F32),
            pltpu.SemaphoreType.DMA((9,)),
            pltpu.SemaphoreType.DMA((2,)),
        ],
        compiler_params=WHOLE,
        cost_estimate=pl.CostEstimate(flops=10**9, bytes_accessed=5000000, transcendentals=200000),
    )(*args, *([] if early_call else previous))


def p_side(args, previous):
    n = len(args)
    return pl.pallas_call(
        p_kernel,
        out_shape=(GRAD, GRAD),
        in_specs=[SMEM, SMEM] + [HBM] * n,
        out_specs=(HBM, HBM),
        input_output_aliases={n: 0, n + 1: 1},
        scratch_shapes=[
            pltpu.VMEM((4 * ROWS, D), BF16),
            pltpu.VMEM((ROWS, D), BF16),
            pltpu.VMEM((ROWS, 4 * ROWS), BF16),
            pltpu.VMEM((ROWS, D), BF16),
            pltpu.VMEM((ROWS, D), F32),
            pltpu.SemaphoreType.DMA((9,)),
            pltpu.SemaphoreType.DMA,
        ],
        compiler_params=WHOLE,
        cost_estimate=pl.CostEstimate(flops=10**9, bytes_accessed=5000000, transcendentals=200000),
    )(*args, *previous)


def body(image, text, e, b):
    bar = lax.optimization_barrier
    p0, q0 = units(image, text)
    p1 = hop(p0, 1)
    d00, d00t, sums = own(e, b, p0, q0)
    q0s, sums = bar((q0, sums))
    q1 = hop(q0s, -1)
    p2 = hop(p1, 1)
    d01, d10, sums = middle(e, b, sums, p0, q0, p1, q1)
    row = last(e, b, sums, q1, p2, 64)
    row, q1s, p2s = bar((row, q1, p2))
    q2 = hop(q1s, -1)
    p3 = hop(p2s, 1)
    row = lax.all_to_all(row, ("x", "y", "c"), 0, 0, tiled=True)
    row, q2s = bar((row, q2))
    q3 = hop(q2s, -1)
    row = jnp.sum(row, axis=0, keepdims=True)
    q_args = (e, b, image, text, p0, p1, p2, p3, q0, q2s, d00, d01)
    row, done = bar((row, q_side(q_args, None)))
    row = lax.all_to_all(jnp.broadcast_to(row, (12, 128)), ("l", "h"), 0, 0, tiled=True)
    row, done = bar((row, done))
    totals = jnp.sum(row, axis=0)[:3] / jnp.float32(ROWS * N_BLK * N_GRP)
    grad_image, grad_text, d20 = q_side(q_args, done)
    p_args = (e, b, image, text, q0, q1, q2s, q3, p0, d00t, d10, d20)
    grad_image, grad_text = p_side(p_args, (grad_image, grad_text))
    return grad_image, grad_text, totals


def solution(mesh):
    fine = Mesh(mesh.devices.reshape(BLK_PARTS + GRP_PARTS), AXES)
    split = P(AXES, None)
    return jax.shard_map(
        body,
        mesh=fine,
        in_specs=(split, split, P(), P()),
        out_specs=(split, split, P()),
        check_vma=False,
    )
```

```python
import functools

import jax
import jax.numpy as jnp
from jax import lax
from jax.experimental import pallas as pl
from jax.experimental.pallas import tpu as pltpu
from jax.sharding import Mesh, PartitionSpec as P

EPSILON = 1e-06
ROWS, D = 256, 1152
BLK_PARTS = (4, 3, 8)
GRP_PARTS = (4, 2)
N_BLK, N_GRP = 96, 8
AXES = ("x", "l", "y", "h", "c")
BF16, F32 = jnp.bfloat16, jnp.float32
PARAMS = pltpu.CompilerParams(vmem_limit_bytes=16 * 1024 * 1024)
LIGHT = pl.CostEstimate(flops=1000, bytes_accessed=1000, transcendentals=0)
WHOLE = pltpu.CompilerParams(vmem_limit_bytes=60 * 1024 * 1024)
CHUNK = 32
GRAD = jax.ShapeDtypeStruct((ROWS, D), F32)
EARLY_PLANES = 5

SMEM = pl.BlockSpec(memory_space=pltpu.SMEM)
VMEM = pl.BlockSpec(memory_space=pltpu.VMEM)
HBM = pl.BlockSpec(memory_space=pltpu.HBM)


def hop(value, steps):
    pairs = []
    for b in range(N_BLK):
        for g in range(N_GRP):
            way = steps if g % 2 == 0 else -steps
            pairs.append((b * N_GRP + g, ((b + way) % N_BLK) * N_GRP + g))
    return lax.ppermute(value, AXES, pairs)


def cosines(rows, cols):
    return lax.dot_general(rows, cols, (((1,), (1,)), ((), ())), preferred_element_type=F32)


def sigmoid_parts(x):
    small = jnp.exp(-jnp.abs(x))
    return small, jnp.where(x >= 0, 1.0, small) / (1.0 + small)


def folded(values):
    part = values[0:8]
    for r in range(8, ROWS, 8):
        part = part + values[r : r + 8]
    return part[:, 0:128] + part[:, 128:256]


def add_sums(sums_ref, cosine, logit, x, slope, small):
    softplus = jnp.maximum(x, 0.0) + jnp.log1p(small)
    sums_ref[0:8, :] += folded(softplus)
    sums_ref[8:16, :] += folded(slope * cosine)
    sums_ref[16:24, :] += folded(slope)


def logits(cosine, e_ref, b_ref):
    scale = jnp.exp(jnp.full((1, ROWS), e_ref[0], F32))
    return scale * cosine + b_ref[0]


PART = 64


def to_unit(source, out):
    for r in range(0, ROWS, CHUNK):
        v = source[r : r + CHUNK, :].astype(F32)
        inverse = lax.rsqrt(jnp.sum(v * v, axis=-1, keepdims=True) + EPSILON)
        out[r : r + CHUNK, :] = (v * inverse).astype(BF16)


def unit_kernel(image, text, p0, q0):
    even = lax.axis_index("c") == 0

    @pl.when(even)
    def _():
        to_unit(text, p0)
        to_unit(image, q0)

    @pl.when(jnp.logical_not(even))
    def _():
        to_unit(image, p0)
        to_unit(text, q0)


def units(image, text):
    rows = jax.ShapeDtypeStruct((ROWS, D), BF16)
    return pl.pallas_call(
        unit_kernel,
        out_shape=(rows, rows),
        in_specs=[VMEM, VMEM],
        out_specs=(VMEM, VMEM),
        compiler_params=PARAMS,
        cost_estimate=LIGHT,
    )(image, text)


def own_kernel(e_ref, b_ref, p0, q0, d00, d00t, sums):
    i = lax.broadcasted_iota(jnp.int32, (ROWS, ROWS), 0)
    j = lax.broadcasted_iota(jnp.int32, (ROWS, ROWS), 1)
    pair = i == j
    sums[...] = jnp.zeros_like(sums)
    cosine = cosines(q0[...], p0[...])
    logit = logits(cosine, e_ref, b_ref)
    x = jnp.where(pair, -logit, logit)
    small, sig = sigmoid_parts(x)
    slope = jnp.where(pair, -sig, sig)
    add_sums(sums, cosine, logit, x, slope, small)
    d00[...] = slope.astype(BF16)
    logit = logits(cosines(p0[...], q0[...]), e_ref, b_ref)
    _, sig = sigmoid_parts(jnp.where(pair, -logit, logit))
    d00t[...] = jnp.where(pair, -sig, sig).astype(BF16)


def own(e, b, p0, q0):
    return pl.pallas_call(
        own_kernel,
        out_shape=(
            jax.ShapeDtypeStruct((ROWS, ROWS), BF16),
            jax.ShapeDtypeStruct((ROWS, ROWS), BF16),
            jax.ShapeDtypeStruct((24, 128), F32),
        ),
        in_specs=[SMEM, SMEM, VMEM, VMEM],
        out_specs=(VMEM, VMEM, VMEM),
        compiler_params=PARAMS,
        cost_estimate=LIGHT,
    )(e, b, p0, q0)


def grid_sums(e_ref, b_ref, rows, cols, sums):
    cosine = cosines(rows, cols)
    logit = logits(cosine, e_ref, b_ref)
    small, slope = sigmoid_parts(logit)
    add_sums(sums, cosine, logit, logit, slope, small)
    return slope.astype(BF16)


def middle_kernel(e_ref, b_ref, sums_in, p0, q0, p1, q1, d00, d00t, sums, g_q, g_p):
    sums[...] = sums_in[...]
    d01 = grid_sums(e_ref, b_ref, q0[...], p1[...], sums)
    grid_sums(e_ref, b_ref, q1[...], p1[...], sums)
    g_q[...] = jnp.dot(d00[...], p0[...], preferred_element_type=F32)
    g_q[...] += jnp.dot(d01, p1[...], preferred_element_type=F32)
    d10 = slope_block(e_ref, b_ref, p0[...], q1[...])
    g_p[...] = jnp.dot(d00t[...], q0[...], preferred_element_type=F32)
    g_p[...] += jnp.dot(d10, q1[...], preferred_element_type=F32)


def middle(e, b, sums, p0, q0, p1, q1, d00, d00t):
    return pl.pallas_call(
        middle_kernel,
        out_shape=(jax.ShapeDtypeStruct((24, 128), F32), GRAD, GRAD),
        in_specs=[SMEM, SMEM] + [VMEM] * 7,
        out_specs=(VMEM, VMEM, VMEM),
        compiler_params=PARAMS,
        cost_estimate=LIGHT,
    )(e, b, sums, p0, q0, p1, q1, d00, d00t)


def last_kernel(e_ref, b_ref, sums_in, q1, p2, out, sums):
    sums[...] = sums_in[...]
    grid_sums(e_ref, b_ref, q1[...], p2[...], sums)
    scale = jnp.exp(jnp.full((1, 1), e_ref[0], F32))
    loss = jnp.sum(sums[0:8, :], keepdims=True)
    by_scale = scale * jnp.sum(sums[8:16, :], keepdims=True)
    by_bias = jnp.sum(sums[16:24, :], keepdims=True)
    lane = lax.broadcasted_iota(jnp.int32, out.shape, 1)
    row = jnp.where(lane == 0, loss, jnp.where(lane == 1, by_scale, jnp.where(lane == 2, by_bias, 0.0)))
    out[...] = row


def last(e, b, sums, q1, p2, count):
    return pl.pallas_call(
        last_kernel,
        out_shape=jax.ShapeDtypeStruct((count, 128), F32),
        in_specs=[SMEM, SMEM] + [VMEM] * 3,
        out_specs=VMEM,
        scratch_shapes=[pltpu.VMEM((24, 128), F32)],
        compiler_params=PARAMS,
        cost_estimate=LIGHT,
    )(e, b, sums, q1, p2)


def started(pairs, sems):
    copies = [pltpu.make_async_copy(src, dst, sems.at[n]) for n, (src, dst) in enumerate(pairs)]
    for copy in copies:
        copy.start()
    return copies


def either(chosen, first, second):
    @pl.when(chosen)
    def _():
        first.start()

    @pl.when(jnp.logical_not(chosen))
    def _():
        second.start()


def inverse_norm(v):
    return lax.rsqrt(jnp.sum(v * v, axis=-1, keepdims=True) + EPSILON)


def finish(e_ref, total, raw, out, is_text, out_image, out_text, sem):
    scale = jnp.exp(jnp.full((1, 1), e_ref[0], F32))
    for r in range(0, ROWS, CHUNK):
        rows = slice(r, r + CHUNK)
        v = raw[rows, :].astype(F32)
        inverse = inverse_norm(v)
        u = v * inverse
        g = scale * total[rows, :]
        out[rows, :] = inverse * (g - u * jnp.sum(u * g, axis=-1, keepdims=True))
        if (r + CHUNK) % PART == 0:
            part = pl.ds(r + CHUNK - PART, PART)
            either(
                is_text,
                pltpu.make_async_copy(out.at[part, :], out_text.at[part, :], sem),
                pltpu.make_async_copy(out.at[part, :], out_image.at[part, :], sem),
            )


def slope_block(e_ref, b_ref, rows, cols):
    return sigmoid_parts(logits(cosines(rows, cols), e_ref, b_ref))[1].astype(BF16)


def load_raw(is_text, image, text, raw, sem):
    from_text = pltpu.make_async_copy(text, raw, sem)
    either(is_text, from_text, pltpu.make_async_copy(image, raw, sem))
    return from_text


def side_kernel(side, when, e_ref, b_ref, image, text, near, far2, far3, *refs):
    out_image, out_text, total, raw, out, own, far, d, sems, out_sem = refs if when == "early" else refs[2:]
    early = 3 * lax.axis_index("h") + lax.axis_index("l") < EARLY_PLANES
    is_text = lax.axis_index("c") == 1 - side

    def work():
        raw_copy = load_raw(is_text, image, text, raw, sems.at[3])
        copies = started([(far2, far.at[pl.ds(0, ROWS), :]), (far3, far.at[pl.ds(ROWS, ROWS), :]), (near, total)], sems)
        raw_copy.wait()
        for r in range(0, ROWS, CHUNK):
            v = raw[r : r + CHUNK, :].astype(F32)
            own[r : r + CHUNK, :] = (v * inverse_norm(v)).astype(BF16)
        for n in range(2):
            copies[n].wait()
            rows = pl.ds(n * ROWS, ROWS)
            d[:, rows] = slope_block(e_ref, b_ref, own[...], far[rows, :])
        copies[2].wait()
        total[...] += jnp.dot(d[...], far[...], preferred_element_type=F32)
        finish(e_ref, total, raw, out, is_text, out_image, out_text, out_sem)
        pltpu.make_async_copy(out, out_text, out_sem).wait()

    if when == "always":
        work()
    else:
        pl.when(early if when == "early" else jnp.logical_not(early))(work)


def one_side(side, when, args, previous=()):
    n = len(args)
    return pl.pallas_call(
        functools.partial(side_kernel, side, when),
        out_shape=(GRAD, GRAD),
        in_specs=[SMEM, SMEM] + [HBM] * (n - 2 + len(previous)),
        out_specs=(HBM, HBM),
        input_output_aliases={n: 0, n + 1: 1} if previous else {},
        scratch_shapes=[
            pltpu.VMEM((ROWS, D), F32),
            pltpu.VMEM((ROWS, D), BF16),
            pltpu.VMEM((ROWS, D), F32),
            pltpu.VMEM((ROWS, D), BF16),
            pltpu.VMEM((2 * ROWS, D), BF16),
            pltpu.VMEM((ROWS, 2 * ROWS), BF16),
            pltpu.SemaphoreType.DMA((4,)),
            pltpu.SemaphoreType.DMA,
        ],
        compiler_params=WHOLE,
        cost_estimate=LIGHT,
    )(*args, *previous)


def body(image, text, e, b):
    bar = lax.optimization_barrier
    p0, q0 = units(image, text)
    p1 = hop(p0, 1)
    d00, d00t, sums = own(e, b, p0, q0)
    sums, q0s = bar((sums, q0))
    q1 = hop(q0s, -1)
    p2 = hop(p1, 1)
    sums, g_q, g_p = middle(e, b, sums, p0, q0, p1, q1, d00, d00t)
    sums, q1s = bar((sums, q1))
    q2 = hop(q1s, -1)
    row = last(e, b, sums, q1, p2, 64)
    row, p2s = bar((row, p2))
    p3 = hop(p2s, 1)
    row = lax.all_to_all(row, ("x", "y", "c"), 0, 0, tiled=True)
    row, q2 = bar((row, q2))
    q3 = hop(q2, -1)
    row, p3 = bar((jnp.sum(row, axis=0, keepdims=True), p3))
    q_args = (e, b, image, text, g_q, p2, p3)
    row, done = bar((row, one_side(0, "early", q_args)))
    row = lax.all_to_all(jnp.broadcast_to(row, (12, 128)), ("l", "h"), 0, 0, tiled=True)
    row, done = bar((row, done))
    totals = jnp.sum(row, axis=0)[:3] / jnp.float32(ROWS * N_BLK * N_GRP)
    done = one_side(0, "late", q_args, done)
    grad_image, grad_text = one_side(1, "always", (e, b, image, text, g_p, q2, q3), done)
    return grad_image, grad_text, totals


def solution(mesh):
    fine = Mesh(mesh.devices.reshape(BLK_PARTS + GRP_PARTS), AXES)
    split = P(AXES, None)
    return jax.shard_map(
        body,
        mesh=fine,
        in_specs=(split, split, P(), P()),
        out_specs=(split, split, P()),
        check_vma=False,
    )
```

```python
import functools

import jax
import jax.numpy as jnp
from jax import lax
from jax.experimental import pallas as pl
from jax.experimental.pallas import tpu as pltpu
from jax.sharding import Mesh, PartitionSpec as P

EPSILON = 1e-06
ROWS, D = 256, 1152
BLK_PARTS = (4, 3, 8)
GRP_PARTS = (4, 2)
N_BLK, N_GRP = 96, 8
AXES = ("x", "l", "y", "h", "c")
BF16, F32 = jnp.bfloat16, jnp.float32
PARAMS = pltpu.CompilerParams(vmem_limit_bytes=16 * 1024 * 1024)
LIGHT = pl.CostEstimate(flops=1000, bytes_accessed=1000, transcendentals=0)
WHOLE = pltpu.CompilerParams(vmem_limit_bytes=62 * 1024 * 1024)
CHUNK = 32
GRAD = jax.ShapeDtypeStruct((ROWS, D), F32)
EARLY_PLANES = 5

SMEM = pl.BlockSpec(memory_space=pltpu.SMEM)
VMEM = pl.BlockSpec(memory_space=pltpu.VMEM)
HBM = pl.BlockSpec(memory_space=pltpu.HBM)


def hop(value, steps):
    pairs = []
    for b in range(N_BLK):
        for g in range(N_GRP):
            way = steps if g % 2 == 0 else -steps
            pairs.append((b * N_GRP + g, ((b + way) % N_BLK) * N_GRP + g))
    return lax.ppermute(value, AXES, pairs)


def cosines(rows, cols):
    return lax.dot_general(rows, cols, (((1,), (1,)), ((), ())), preferred_element_type=F32)


def sigmoid_parts(x):
    small = jnp.exp(-jnp.abs(x))
    return small, jnp.where(x >= 0, 1.0, small) / (1.0 + small)


def folded(values):
    part = values[0:8]
    for r in range(8, ROWS, 8):
        part = part + values[r : r + 8]
    return part[:, 0:128] + part[:, 128:256]


def add_sums(sums_ref, cosine, logit, x, slope, small):
    softplus = jnp.maximum(x, 0.0) + jnp.log1p(small)
    sums_ref[0:8, :] += folded(softplus)
    sums_ref[8:16, :] += folded(slope * cosine)
    sums_ref[16:24, :] += folded(slope)


def logits(cosine, e_ref, b_ref):
    scale = jnp.exp(jnp.full((1, ROWS), e_ref[0], F32))
    return scale * cosine + b_ref[0]


PART = 64


def to_unit(source, out):
    for r in range(0, ROWS, CHUNK):
        v = source[r : r + CHUNK, :].astype(F32)
        inverse = lax.rsqrt(jnp.sum(v * v, axis=-1, keepdims=True) + EPSILON)
        out[r : r + CHUNK, :] = (v * inverse).astype(BF16)


def unit_kernel(image, text, p0, q0):
    even = lax.axis_index("c") == 0

    @pl.when(even)
    def _():
        to_unit(text, p0)
        to_unit(image, q0)

    @pl.when(jnp.logical_not(even))
    def _():
        to_unit(image, p0)
        to_unit(text, q0)


def units(image, text):
    rows = jax.ShapeDtypeStruct((ROWS, D), BF16)
    return pl.pallas_call(
        unit_kernel,
        out_shape=(rows, rows),
        in_specs=[VMEM, VMEM],
        out_specs=(VMEM, VMEM),
        compiler_params=PARAMS,
        cost_estimate=LIGHT,
    )(image, text)


def own_kernel(e_ref, b_ref, p0, q0, d00, d00t, sums):
    i = lax.broadcasted_iota(jnp.int32, (ROWS, ROWS), 0)
    j = lax.broadcasted_iota(jnp.int32, (ROWS, ROWS), 1)
    pair = i == j
    sums[...] = jnp.zeros_like(sums)
    cosine = cosines(q0[...], p0[...])
    logit = logits(cosine, e_ref, b_ref)
    x = jnp.where(pair, -logit, logit)
    small, sig = sigmoid_parts(x)
    slope = jnp.where(pair, -sig, sig)
    add_sums(sums, cosine, logit, x, slope, small)
    d00[...] = slope.astype(BF16)
    logit = logits(cosines(p0[...], q0[...]), e_ref, b_ref)
    _, sig = sigmoid_parts(jnp.where(pair, -logit, logit))
    d00t[...] = jnp.where(pair, -sig, sig).astype(BF16)


def own(e, b, p0, q0):
    return pl.pallas_call(
        own_kernel,
        out_shape=(
            jax.ShapeDtypeStruct((ROWS, ROWS), BF16),
            jax.ShapeDtypeStruct((ROWS, ROWS), BF16),
            jax.ShapeDtypeStruct((24, 128), F32),
        ),
        in_specs=[SMEM, SMEM, VMEM, VMEM],
        out_specs=(VMEM, VMEM, VMEM),
        compiler_params=PARAMS,
        cost_estimate=LIGHT,
    )(e, b, p0, q0)


def grid_sums(e_ref, b_ref, rows, cols, sums):
    cosine = cosines(rows, cols)
    logit = logits(cosine, e_ref, b_ref)
    small, slope = sigmoid_parts(logit)
    add_sums(sums, cosine, logit, logit, slope, small)
    return slope.astype(BF16)


def middle_kernel(e_ref, b_ref, sums_in, p0, q0, p1, q1, d00, d00t, sums, g_q, g_p):
    sums[...] = sums_in[...]
    d01 = grid_sums(e_ref, b_ref, q0[...], p1[...], sums)
    grid_sums(e_ref, b_ref, q1[...], p1[...], sums)
    g_q[...] = jnp.dot(d00[...], p0[...], preferred_element_type=F32)
    g_q[...] += jnp.dot(d01, p1[...], preferred_element_type=F32)
    d10 = slope_block(e_ref, b_ref, p0[...], q1[...])
    g_p[...] = jnp.dot(d00t[...], q0[...], preferred_element_type=F32)
    g_p[...] += jnp.dot(d10, q1[...], preferred_element_type=F32)


def middle(e, b, sums, p0, q0, p1, q1, d00, d00t):
    return pl.pallas_call(
        middle_kernel,
        out_shape=(jax.ShapeDtypeStruct((24, 128), F32), GRAD, GRAD),
        in_specs=[SMEM, SMEM] + [VMEM] * 7,
        out_specs=(VMEM, VMEM, VMEM),
        compiler_params=PARAMS,
        cost_estimate=LIGHT,
    )(e, b, sums, p0, q0, p1, q1, d00, d00t)


def last_kernel(e_ref, b_ref, sums_in, q1, p2, out, sums):
    sums[...] = sums_in[...]
    grid_sums(e_ref, b_ref, q1[...], p2[...], sums)
    share = 1.0 / (ROWS * N_BLK * N_GRP)
    scale = jnp.exp(jnp.full((1, 1), e_ref[0], F32))
    loss = share * jnp.sum(sums[0:8, :], keepdims=True)
    by_scale = share * scale * jnp.sum(sums[8:16, :], keepdims=True)
    by_bias = share * jnp.sum(sums[16:24, :], keepdims=True)
    lane = lax.broadcasted_iota(jnp.int32, out.shape, 1)
    row = jnp.where(lane == 0, loss, jnp.where(lane == 1, by_scale, jnp.where(lane == 2, by_bias, 0.0)))
    out[...] = row


def last(e, b, sums, q1, p2, count):
    return pl.pallas_call(
        last_kernel,
        out_shape=jax.ShapeDtypeStruct((count, 128), F32),
        in_specs=[SMEM, SMEM] + [VMEM] * 3,
        out_specs=VMEM,
        scratch_shapes=[pltpu.VMEM((24, 128), F32)],
        compiler_params=PARAMS,
        cost_estimate=LIGHT,
    )(e, b, sums, q1, p2)


def started(pairs, sems):
    copies = [pltpu.make_async_copy(src, dst, sems.at[n]) for n, (src, dst) in enumerate(pairs)]
    for copy in copies:
        copy.start()
    return copies


def either(chosen, first, second):
    @pl.when(chosen)
    def _():
        first.start()

    @pl.when(jnp.logical_not(chosen))
    def _():
        second.start()


def inverse_norm(v):
    return lax.rsqrt(jnp.sum(v * v, axis=-1, keepdims=True) + EPSILON)


def finish(e_ref, total, raw, out, is_text, out_image, out_text, sem):
    scale = jnp.exp(jnp.full((1, 1), e_ref[0], F32))
    for r in range(0, ROWS, CHUNK):
        rows = slice(r, r + CHUNK)
        v = raw[rows, :].astype(F32)
        inverse = inverse_norm(v)
        u = v * inverse
        g = scale * total[rows, :]
        out[rows, :] = inverse * (g - u * jnp.sum(u * g, axis=-1, keepdims=True))
        if (r + CHUNK) % PART == 0:
            part = pl.ds(r + CHUNK - PART, PART)
            either(
                is_text,
                pltpu.make_async_copy(out.at[part, :], out_text.at[part, :], sem),
                pltpu.make_async_copy(out.at[part, :], out_image.at[part, :], sem),
            )


def slope_block(e_ref, b_ref, rows, cols):
    return sigmoid_parts(logits(cosines(rows, cols), e_ref, b_ref))[1].astype(BF16)


def load_raw(is_text, image, text, raw, sem):
    from_text = pltpu.make_async_copy(text, raw, sem)
    either(is_text, from_text, pltpu.make_async_copy(image, raw, sem))
    return from_text


def side_kernel(side, when, e_ref, b_ref, image, text, near, far2, far3, *refs):
    out_image, out_text, total, raw, out, own, far, d, sems, out_sem = refs if when == "early" else refs[2:]
    early = 3 * lax.axis_index("h") + lax.axis_index("l") < EARLY_PLANES
    is_text = lax.axis_index("c") == 1 - side

    def work():
        raw_copy = load_raw(is_text, image, text, raw, sems.at[3])
        copies = started([(far2, far.at[pl.ds(0, ROWS), :]), (far3, far.at[pl.ds(ROWS, ROWS), :]), (near, total)], sems)
        raw_copy.wait()
        for r in range(0, ROWS, CHUNK):
            v = raw[r : r + CHUNK, :].astype(F32)
            own[r : r + CHUNK, :] = (v * inverse_norm(v)).astype(BF16)
        for n in range(2):
            copies[n].wait()
            rows = pl.ds(n * ROWS, ROWS)
            d[:, rows] = slope_block(e_ref, b_ref, own[...], far[rows, :])
        copies[2].wait()
        total[...] += jnp.dot(d[...], far[...], preferred_element_type=F32)
        finish(e_ref, total, raw, out, is_text, out_image, out_text, out_sem)
        pltpu.make_async_copy(out, out_text, out_sem).wait()

    if when == "always":
        work()
    else:
        pl.when(early if when == "early" else jnp.logical_not(early))(work)


def one_side(side, when, args, previous=()):
    n = len(args)
    return pl.pallas_call(
        functools.partial(side_kernel, side, when),
        out_shape=(GRAD, GRAD),
        in_specs=[SMEM, SMEM] + [HBM] * (n - 2 + len(previous)),
        out_specs=(HBM, HBM),
        input_output_aliases={n: 0, n + 1: 1} if previous else {},
        scratch_shapes=[
            pltpu.VMEM((ROWS, D), F32),
            pltpu.VMEM((ROWS, D), BF16),
            pltpu.VMEM((ROWS, D), F32),
            pltpu.VMEM((ROWS, D), BF16),
            pltpu.VMEM((2 * ROWS, D), BF16),
            pltpu.VMEM((ROWS, 2 * ROWS), BF16),
            pltpu.SemaphoreType.DMA((4,)),
            pltpu.SemaphoreType.DMA,
        ],
        compiler_params=WHOLE,
        cost_estimate=LIGHT,
    )(*args, *previous)


def body(image, text, e, b):
    bar = lax.optimization_barrier
    p0, q0 = units(image, text)
    p1 = hop(p0, 1)
    d00, d00t, sums = own(e, b, p0, q0)
    sums, q0s = bar((sums, q0))
    q1 = hop(q0s, -1)
    p2 = hop(p1, 1)
    sums, g_q, g_p = middle(e, b, sums, p0, q0, p1, q1, d00, d00t)
    sums, q1s = bar((sums, q1))
    q2 = hop(q1s, -1)
    row = last(e, b, sums, q1, p2, 16)
    row, p2s = bar((row, p2))
    p3 = hop(p2s, 1)
    row = lax.all_to_all(row, ("y", "c"), 0, 0, tiled=True)
    row, q2 = bar((row, q2))
    q3 = hop(q2, -1)
    row, p3 = bar((jnp.sum(row, axis=0, keepdims=True), p3))
    q_args = (e, b, image, text, g_q, p2, p3)
    row, done = bar((row, one_side(0, "early", q_args)))
    row = lax.all_to_all(jnp.broadcast_to(row, (48, 128)), ("x", "l", "h"), 0, 0, tiled=True)
    row, done = bar((row, done))
    totals = jnp.sum(row[:, :3], axis=0)
    done = one_side(0, "late", q_args, done)
    grad_image, grad_text = one_side(1, "always", (e, b, image, text, g_p, q2, q3), done)
    return grad_image, grad_text, totals


def solution(mesh):
    fine = Mesh(mesh.devices.reshape(BLK_PARTS + GRP_PARTS), AXES)
    split = P(AXES, None)
    return jax.shard_map(
        body,
        mesh=fine,
        in_specs=(split, split, P(), P()),
        out_specs=(split, split, P()),
        check_vma=False,
    )
```

```python
import functools

import jax
import jax.numpy as jnp
from jax import lax
from jax.experimental import pallas as pl
from jax.experimental.pallas import tpu as pltpu
from jax.sharding import Mesh, PartitionSpec as P

EPSILON = 1e-06
ROWS, D = 256, 1152
BLK_PARTS = (4, 3, 8)
GRP_PARTS = (4, 2)
N_BLK, N_GRP = 96, 8
AXES = ("x", "l", "y", "h", "c")
BF16, F32 = jnp.bfloat16, jnp.float32
PARAMS = pltpu.CompilerParams(vmem_limit_bytes=16 * 1024 * 1024)
LIGHT = pl.CostEstimate(flops=1000, bytes_accessed=1000, transcendentals=0)
WHOLE = pltpu.CompilerParams(vmem_limit_bytes=62 * 1024 * 1024)
CHUNK = 32
GRAD = jax.ShapeDtypeStruct((ROWS, D), F32)
EARLY_PLANES = 5

SMEM = pl.BlockSpec(memory_space=pltpu.SMEM)
VMEM = pl.BlockSpec(memory_space=pltpu.VMEM)
HBM = pl.BlockSpec(memory_space=pltpu.HBM)


def hop(value, steps):
    pairs = []
    for b in range(N_BLK):
        for g in range(N_GRP):
            way = steps if g % 2 == 0 else -steps
            pairs.append((b * N_GRP + g, ((b + way) % N_BLK) * N_GRP + g))
    return lax.ppermute(value, AXES, pairs)


def cosines(rows, cols):
    return lax.dot_general(rows, cols, (((1,), (1,)), ((), ())), preferred_element_type=F32)


def sigmoid_parts(x):
    small = jnp.exp(-jnp.abs(x))
    return small, jnp.where(x >= 0, 1.0, small) / (1.0 + small)


def folded(values):
    part = values[0:8]
    for r in range(8, ROWS, 8):
        part = part + values[r : r + 8]
    return part[:, 0:128] + part[:, 128:256]


def add_sums(sums_ref, cosine, logit, x, slope, small):
    softplus = jnp.maximum(x, 0.0) + jnp.log1p(small)
    sums_ref[0:8, :] += folded(softplus)
    sums_ref[8:16, :] += folded(slope * cosine)
    sums_ref[16:24, :] += folded(slope)


def logits(cosine, e_ref, b_ref):
    scale = jnp.exp(jnp.full((1, ROWS), e_ref[0], F32))
    return scale * cosine + b_ref[0]


PART = 64


def to_unit(source, out):
    for r in range(0, ROWS, CHUNK):
        v = source[r : r + CHUNK, :].astype(F32)
        inverse = lax.rsqrt(jnp.sum(v * v, axis=-1, keepdims=True) + EPSILON)
        out[r : r + CHUNK, :] = (v * inverse).astype(BF16)


def unit_kernel(image, text, p0, q0):
    even = lax.axis_index("c") == 0

    @pl.when(even)
    def _():
        to_unit(text, p0)
        to_unit(image, q0)

    @pl.when(jnp.logical_not(even))
    def _():
        to_unit(image, p0)
        to_unit(text, q0)


def units(image, text):
    rows = jax.ShapeDtypeStruct((ROWS, D), BF16)
    return pl.pallas_call(
        unit_kernel,
        out_shape=(rows, rows),
        in_specs=[VMEM, VMEM],
        out_specs=(VMEM, VMEM),
        compiler_params=PARAMS,
        cost_estimate=LIGHT,
    )(image, text)


def own_kernel(e_ref, b_ref, p0, q0, d00, d00t, sums):
    i = lax.broadcasted_iota(jnp.int32, (ROWS, ROWS), 0)
    j = lax.broadcasted_iota(jnp.int32, (ROWS, ROWS), 1)
    pair = i == j
    sums[...] = jnp.zeros_like(sums)
    cosine = cosines(q0[...], p0[...])
    logit = logits(cosine, e_ref, b_ref)
    x = jnp.where(pair, -logit, logit)
    small, sig = sigmoid_parts(x)
    slope = jnp.where(pair, -sig, sig)
    add_sums(sums, cosine, logit, x, slope, small)
    d00[...] = slope.astype(BF16)
    logit = logits(cosines(p0[...], q0[...]), e_ref, b_ref)
    _, sig = sigmoid_parts(jnp.where(pair, -logit, logit))
    d00t[...] = jnp.where(pair, -sig, sig).astype(BF16)


def own(e, b, p0, q0):
    return pl.pallas_call(
        own_kernel,
        out_shape=(
            jax.ShapeDtypeStruct((ROWS, ROWS), BF16),
            jax.ShapeDtypeStruct((ROWS, ROWS), BF16),
            jax.ShapeDtypeStruct((24, 128), F32),
        ),
        in_specs=[SMEM, SMEM, VMEM, VMEM],
        out_specs=(VMEM, VMEM, VMEM),
        compiler_params=PARAMS,
        cost_estimate=LIGHT,
    )(e, b, p0, q0)


def grid_sums(e_ref, b_ref, rows, cols, sums):
    cosine = cosines(rows, cols)
    logit = logits(cosine, e_ref, b_ref)
    small, slope = sigmoid_parts(logit)
    add_sums(sums, cosine, logit, logit, slope, small)
    return slope.astype(BF16)


def middle_kernel(e_ref, b_ref, sums_in, p0, q0, p1, q1, d00, d00t, sums, g_q, g_p):
    sums[...] = sums_in[...]
    d01 = grid_sums(e_ref, b_ref, q0[...], p1[...], sums)
    grid_sums(e_ref, b_ref, q1[...], p1[...], sums)
    g_q[...] = jnp.dot(d00[...], p0[...], preferred_element_type=F32)
    g_q[...] += jnp.dot(d01, p1[...], preferred_element_type=F32)
    d10 = slope_block(e_ref, b_ref, p0[...], q1[...])
    g_p[...] = jnp.dot(d00t[...], q0[...], preferred_element_type=F32)
    g_p[...] += jnp.dot(d10, q1[...], preferred_element_type=F32)


def middle(e, b, sums, p0, q0, p1, q1, d00, d00t):
    return pl.pallas_call(
        middle_kernel,
        out_shape=(jax.ShapeDtypeStruct((24, 128), F32), GRAD, GRAD),
        in_specs=[SMEM, SMEM] + [VMEM] * 7,
        out_specs=(VMEM, VMEM, VMEM),
        compiler_params=PARAMS,
        cost_estimate=LIGHT,
    )(e, b, sums, p0, q0, p1, q1, d00, d00t)


def last_kernel(e_ref, b_ref, sums_in, q1, p2, out, sums):
    sums[...] = sums_in[...]
    grid_sums(e_ref, b_ref, q1[...], p2[...], sums)
    share = 1.0 / (ROWS * N_BLK * N_GRP)
    scale = jnp.exp(jnp.full((1, 1), e_ref[0], F32))
    loss = share * jnp.sum(sums[0:8, :], keepdims=True)
    by_scale = share * scale * jnp.sum(sums[8:16, :], keepdims=True)
    by_bias = share * jnp.sum(sums[16:24, :], keepdims=True)
    lane = lax.broadcasted_iota(jnp.int32, out.shape, 1)
    row = jnp.where(lane == 0, loss, jnp.where(lane == 1, by_scale, jnp.where(lane == 2, by_bias, 0.0)))
    out[...] = row


def last(e, b, sums, q1, p2, count):
    return pl.pallas_call(
        last_kernel,
        out_shape=jax.ShapeDtypeStruct((count, 128), F32),
        in_specs=[SMEM, SMEM] + [VMEM] * 3,
        out_specs=VMEM,
        scratch_shapes=[pltpu.VMEM((24, 128), F32)],
        compiler_params=PARAMS,
        cost_estimate=LIGHT,
    )(e, b, sums, q1, p2)


def started(pairs, sems):
    copies = [pltpu.make_async_copy(src, dst, sems.at[n]) for n, (src, dst) in enumerate(pairs)]
    for copy in copies:
        copy.start()
    return copies


def either(chosen, first, second):
    @pl.when(chosen)
    def _():
        first.start()

    @pl.when(jnp.logical_not(chosen))
    def _():
        second.start()


def inverse_norm(v):
    return lax.rsqrt(jnp.sum(v * v, axis=-1, keepdims=True) + EPSILON)


def finish(e_ref, total, raw, out, is_text, out_image, out_text, sem):
    scale = jnp.exp(jnp.full((1, 1), e_ref[0], F32))
    for r in range(0, ROWS, CHUNK):
        rows = slice(r, r + CHUNK)
        v = raw[rows, :].astype(F32)
        inverse = inverse_norm(v)
        u = v * inverse
        g = scale * total[rows, :]
        out[rows, :] = inverse * (g - u * jnp.sum(u * g, axis=-1, keepdims=True))
        if (r + CHUNK) % PART == 0:
            part = pl.ds(r + CHUNK - PART, PART)
            either(
                is_text,
                pltpu.make_async_copy(out.at[part, :], out_text.at[part, :], sem),
                pltpu.make_async_copy(out.at[part, :], out_image.at[part, :], sem),
            )


def slope_block(e_ref, b_ref, rows, cols):
    return sigmoid_parts(logits(cosines(rows, cols), e_ref, b_ref))[1].astype(BF16)


def load_raw(is_text, image, text, raw, sem):
    from_text = pltpu.make_async_copy(text, raw, sem)
    either(is_text, from_text, pltpu.make_async_copy(image, raw, sem))
    return from_text


def unit_rows(raw, own):
    for r in range(0, ROWS, CHUNK):
        v = raw[r : r + CHUNK, :].astype(F32)
        own[r : r + CHUNK, :] = (v * inverse_norm(v)).astype(BF16)


def q_kernel(when, e_ref, b_ref, image, text, g_q, p2, p3, g_p, q2, *refs):
    out_image, out_text, out_p, total, raw, out, own, far, d, total_p, raw_p, far_p, sems, out_sems = (
        refs if when == "early" else refs[3:]
    )
    early = 3 * lax.axis_index("h") + lax.axis_index("l") < EARLY_PLANES
    q_text = lax.axis_index("c") == 1
    p_text = lax.axis_index("c") == 0

    @pl.when(early if when == "early" else jnp.logical_not(early))
    def _():
        raw_copy = load_raw(q_text, image, text, raw, sems.at[5])
        copies = started(
            [(p2, far.at[pl.ds(0, ROWS), :]), (p3, far.at[pl.ds(ROWS, ROWS), :]), (g_q, total), (q2, far_p), (g_p, total_p)],
            sems,
        )
        raw_p_copy = load_raw(p_text, image, text, raw_p, sems.at[6])
        raw_copy.wait()
        unit_rows(raw, own)
        for n in range(2):
            copies[n].wait()
            rows = pl.ds(n * ROWS, ROWS)
            d[:, rows] = slope_block(e_ref, b_ref, own[...], far[rows, :])
        copies[2].wait()
        total[...] += jnp.dot(d[...], far[...], preferred_element_type=F32)
        finish(e_ref, total, raw, out, q_text, out_image, out_text, out_sems.at[0])
        raw_p_copy.wait()
        unit_rows(raw_p, own)
        copies[3].wait()
        slopes = slope_block(e_ref, b_ref, own[...], far_p[...])
        copies[4].wait()
        total_p[...] += jnp.dot(slopes, far_p[...], preferred_element_type=F32)
        store = pltpu.make_async_copy(total_p, out_p, out_sems.at[1])
        store.start()
        store.wait()
        pltpu.make_async_copy(out, out_text, out_sems.at[0]).wait()


def q_side(when, args, previous=()):
    n = len(args)
    return pl.pallas_call(
        functools.partial(q_kernel, when),
        out_shape=(GRAD, GRAD, GRAD),
        in_specs=[SMEM, SMEM] + [HBM] * (n - 2 + len(previous)),
        out_specs=(HBM, HBM, HBM),
        input_output_aliases={n: 0, n + 1: 1, n + 2: 2} if previous else {},
        scratch_shapes=[
            pltpu.VMEM((ROWS, D), F32),
            pltpu.VMEM((ROWS, D), BF16),
            pltpu.VMEM((ROWS, D), F32),
            pltpu.VMEM((ROWS, D), BF16),
            pltpu.VMEM((2 * ROWS, D), BF16),
            pltpu.VMEM((ROWS, 2 * ROWS), BF16),
            pltpu.VMEM((ROWS, D), F32),
            pltpu.VMEM((ROWS, D), BF16),
            pltpu.VMEM((ROWS, D), BF16),
            pltpu.SemaphoreType.DMA((7,)),
            pltpu.SemaphoreType.DMA((2,)),
        ],
        compiler_params=WHOLE,
        cost_estimate=LIGHT,
    )(*args, *previous)


def p_kernel(e_ref, b_ref, image, text, g_p, q3, *refs):
    _, _, out_image, out_text, total, raw, out, own, far, sems, out_sem = refs
    is_text = lax.axis_index("c") == 0
    raw_copy = load_raw(is_text, image, text, raw, sems.at[2])
    copies = started([(q3, far), (g_p, total)], sems)
    raw_copy.wait()
    unit_rows(raw, own)
    copies[0].wait()
    slopes = slope_block(e_ref, b_ref, own[...], far[...])
    copies[1].wait()
    total[...] += jnp.dot(slopes, far[...], preferred_element_type=F32)
    finish(e_ref, total, raw, out, is_text, out_image, out_text, out_sem)
    pltpu.make_async_copy(out, out_text, out_sem).wait()


def p_side(args, previous):
    n = len(args)
    return pl.pallas_call(
        p_kernel,
        out_shape=(GRAD, GRAD),
        in_specs=[SMEM, SMEM] + [HBM] * n,
        out_specs=(HBM, HBM),
        input_output_aliases={n: 0, n + 1: 1},
        scratch_shapes=[
            pltpu.VMEM((ROWS, D), F32),
            pltpu.VMEM((ROWS, D), BF16),
            pltpu.VMEM((ROWS, D), F32),
            pltpu.VMEM((ROWS, D), BF16),
            pltpu.VMEM((ROWS, D), BF16),
            pltpu.SemaphoreType.DMA((3,)),
            pltpu.SemaphoreType.DMA,
        ],
        compiler_params=WHOLE,
        cost_estimate=LIGHT,
    )(*args, *previous)


def body(image, text, e, b):
    bar = lax.optimization_barrier
    p0, q0 = units(image, text)
    p1 = hop(p0, 1)
    d00, d00t, sums = own(e, b, p0, q0)
    sums, q0s = bar((sums, q0))
    q1 = hop(q0s, -1)
    p2 = hop(p1, 1)
    sums, g_q, g_p = middle(e, b, sums, p0, q0, p1, q1, d00, d00t)
    sums, q1s = bar((sums, q1))
    q2 = hop(q1s, -1)
    row = last(e, b, sums, q1, p2, 16)
    row, p2s = bar((row, p2))
    p3 = hop(p2s, 1)
    row = lax.all_to_all(row, ("y", "c"), 0, 0, tiled=True)
    row, q2 = bar((row, q2))
    q3 = hop(q2, -1)
    row, p3 = bar((jnp.sum(row, axis=0, keepdims=True), p3))
    q_args = (e, b, image, text, g_q, p2, p3, g_p, q2)
    row, done = bar((row, q_side("early", q_args)))
    row = lax.all_to_all(jnp.broadcast_to(row, (48, 128)), ("x", "l", "h"), 0, 0, tiled=True)
    row, done = bar((row, done))
    totals = jnp.sum(row[:, :3], axis=0)
    grad_image, grad_text, g_p = q_side("late", q_args, done)
    grad_image, grad_text = p_side((e, b, image, text, g_p, q3), (grad_image, grad_text))
    return grad_image, grad_text, totals


def solution(mesh):
    fine = Mesh(mesh.devices.reshape(BLK_PARTS + GRP_PARTS), AXES)
    split = P(AXES, None)
    return jax.shard_map(
        body,
        mesh=fine,
        in_specs=(split, split, P(), P()),
        out_specs=(split, split, P()),
        check_vma=False,
    )
```
